512 devices in a mesh: row: 16 (over z_lo, x), col: 32 (over y, z_hi, core).
Axes of the slice: x: 4, y: 8, z: 8 (z_hi: 2, z_lo: 4; z = z_hi * 4 + z_lo), core: 2. Of those that a mesh axis runs over, the one named last changes fastest.
Arguments:
- positions: float32 [3, 32768], P(None, ('row', 'col')), may hold values from -1 to 1
- orient: float32 [2, 32768], P(None, ('row', 'col')), may hold values from -3.140625 to 3.140625
- areas: float32 [32768], P(('row', 'col')), may hold values from 0.008 to 0.16
- incident: float32 [2, 3, 2, 32768], P(None, None, None, ('row', 'col')), may hold values from -6 to 6
- visible: int32 [512, 16, 32], P('row', None, 'col'), may hold values 0 or 1
Outputs:
- currents: float32 [2, 3, 2, 32768], P(None, None, None, ('row', 'col'))
The draws below stay inside these ranges and needn't reach their ends.
All inputs are finite; a program needn't handle non-finite values. No bound on the sum of `visible` on one device may be relied on, other than what follows from the above.
Results may differ from the reference program's by a relative error of at most 0.006.
Values may be sent and summed in bfloat16 or wider, within the bound.
A program may use at most 64 MiB of HBM per device.

```python
import math
import jax
import jax.numpy as jnp
from jax import lax

TILE = 64
POL = 2
ITERS = 3
NF = 32768
TILES = 512
TROWS = 16
TCOLS = 32


def set_ends(drawn, key, smallest, top_value):
    shape = drawn.shape
    spot = [jax.random.randint(jax.random.fold_in(key, axis), (), 0, shape[axis]) for axis in range(len(shape))]
    drawn = drawn.at[tuple(spot)].set(smallest)
    longest = shape.index(max(shape))
    spot[longest] = (spot[longest] + 1) % shape[longest]
    return drawn.at[tuple(spot)].set(top_value)


def level_of(own_key, shape, cuts, smallest, largest):
    factor_of = 1.0
    for dim, parts in cuts:
        draws = jax.random.uniform(jax.random.fold_in(jax.random.fold_in(own_key, 6), dim), (parts,), jnp.float32, smallest / len(cuts), largest / len(cuts))
        factor_of = factor_of * jnp.repeat(jnp.exp(draws), shape[dim] // parts).reshape((-1,) + (1,) * (len(shape) - 1 - dim))
    return factor_of


def centred(key, extent, spread, most, cuts=(), kind=jnp.bfloat16):
    values = jax.random.normal(key, extent, jnp.float32) * spread
    if len(cuts) > 0:
        values = level_of(key, extent, cuts, -0.22, 0.18) * values
    return jnp.clip(values, min=-most, max=most).astype(kind)


def setup_inputs(seed: int = 0) -> dict:
    arg_keys = jax.random.split(jax.random.key(seed), 6)
    positions = jnp.clip(jax.random.uniform(arg_keys[0], (3, NF), jnp.float32, -1.0, 1.0) * level_of(arg_keys[0], (3, NF), ((1, 512),), -0.4, 0.0), -1.0, 1.0)
    orient = jnp.clip(jax.random.uniform(arg_keys[1], (2, NF), jnp.float32, -3.140625, 3.140625), -3.140625, 3.140625)
    areas = jnp.clip(jnp.exp(math.log(0.16) - 2.9957322 * jax.random.uniform(arg_keys[2], (NF,), jnp.float32) ** level_of(arg_keys[2], (NF,), ((0, 512),), -0.2, 0.2)), 0.008, 0.16)
    incident = centred(arg_keys[3], (2, 3, POL, NF), 1.0, 6.0, ((3, 512),), jnp.float32)
    visible = set_ends((jax.random.randint(arg_keys[4], (TILES, TROWS, TCOLS), 0, 4) < 3).astype(jnp.int32), jax.random.fold_in(arg_keys[4], 1), 0, 1)
    return dict(positions=positions, orient=orient, areas=areas, incident=incident, visible=visible)


wave_number = 8.0 * math.pi
soft_square = 0.0025

def normals_from(orient):
    polar_angle = orient[0]
    azimuth = orient[1]
    return jnp.stack([jnp.sin(polar_angle) * jnp.cos(azimuth), jnp.sin(polar_angle) * jnp.sin(azimuth), jnp.cos(polar_angle)])

def right_operand(outgoing, position):
    moments = (position[None, :, None, None, :] * outgoing[:, None].astype(jnp.float32)).astype(jnp.bfloat16)
    stacked = jnp.concatenate([outgoing[:, None], moments], axis=1)
    flattened = stacked.reshape(2, -1, stacked.shape[-1])
    real_part = flattened[0]
    imag_part = flattened[1]
    upper = jnp.concatenate([real_part, -imag_part], axis=1)
    lower = jnp.concatenate([imag_part, real_part], axis=1)
    return jnp.concatenate([upper, lower], axis=0)

def twisted(products, position, normal):
    direct = products[:, 0]
    moments = products[:, 1:]
    normal_dot = lax.optimization_barrier(jnp.sum(normal[None, :, None, :] * direct, axis=1))
    height = lax.optimization_barrier(jnp.sum(normal * position, axis=0))
    twist_part = moments - jnp.swapaxes(moments, 1, 2)
    turned = lax.optimization_barrier(jnp.sum(normal[None, None, :, None, :] * twist_part, axis=2))
    return position[None, :, None, :] * normal_dot[:, None] - height * direct - turned

def kernel_tile(obs_position, visible_pairs, src_position, src_weight):
    separation = obs_position[:, :, None] - src_position[:, None, :]
    dist_square = lax.optimization_barrier(jnp.sum(separation * separation, axis=0)) + soft_square
    distance = jnp.sqrt(dist_square)
    phase_arg = wave_number * distance
    factor = visible_pairs * src_weight[None, :] / (dist_square * distance)
    cosine = jnp.cos(phase_arg)
    sine_part = jnp.sin(phase_arg)
    real_k = factor * (cosine + phase_arg * sine_part)
    imag_k = factor * (phase_arg * cosine - sine_part)
    return jnp.concatenate([real_k, imag_k], axis=1).astype(jnp.bfloat16)

def reference(positions, orient, areas, incident, visible):
    facet_total = positions.shape[1]
    weight_scale = 1.0 / (4.0 * math.pi * math.sqrt(facet_total))
    normal_all = normals_from(orient)
    src_weight = areas * weight_scale
    tile_matrix = visible.reshape(TILES, TILES).astype(jnp.float32)
    column_mask = jnp.repeat(tile_matrix, TILE, axis=1)
    block_len = min(512, facet_total)
    block_count = facet_total // block_len
    tiles_per_block = block_len // TILE
    obs_blocks = positions.reshape(3, block_count, block_len).transpose(1, 0, 2)
    block_ids = jnp.arange(block_count, dtype=jnp.int32)
    current = incident
    for bounce in range(ITERS):
        outgoing = current.astype(jnp.bfloat16)
        operand = right_operand(outgoing, positions)

        def one_block(block_pair):
            obs_position, block_id = block_pair
            rows_mask = lax.dynamic_slice_in_dim(column_mask, block_id * tiles_per_block, tiles_per_block, 0)
            visible_pairs = jnp.repeat(rows_mask, TILE, axis=0)
            tile_now = kernel_tile(obs_position, visible_pairs, positions, src_weight)
            return lax.dot_general(operand, tile_now, (((1,), (1,)), ((), ())), preferred_element_type=jnp.float32)
        blocks = lax.map(one_block, (obs_blocks, block_ids))
        products = blocks.transpose(1, 0, 2).reshape(operand.shape[0], facet_total)
        scattered = twisted(products.reshape(2, 4, 3, POL, facet_total), positions, normal_all)
        current = incident + 2.0 * scattered
    return current
```

```python
import functools
import math

import jax
import jax.numpy as jnp
from jax import lax
from jax.experimental import pallas as pl
from jax.experimental.pallas import tpu as pltpu
from jax.sharding import PartitionSpec as P

ITERS = 3
TILE = 64
MESH = pl.DeviceIdType.MESH
F32, BF16 = jnp.float32, jnp.bfloat16

NX, NY, NZ, NC = 4, 8, 8, 2
Z_ORDER = (0, 1, 7, 2, 6, 3, 5, 4)
NEAR_Z = 5
NOBS = NY * NC * TILE
NSRC = NX * NZ * TILE
NEAR = NEAR_Z * NX * TILE
FAR = NSRC - NEAR
DEPTH = 64
BLOCK = 256
BIG = 2.0**127

YC = tuple((y, c) for y in (4, 3, 5, 2, 6, 1, 7, 0) for c in (1, 0) if y or c)
XZ = tuple(
    (x, z)
    for x, z in sorted(
        ((x, z) for x in range(NX) for z in range(NZ) if x or z),
        key=lambda p: -(min(p[0], NX - p[0]) + min(p[1], NZ - p[1])),
    )
)


def src_slot(x, z):
    return Z_ORDER.index(z % NZ) * NX + x % NX


def split3(v):
    high = v.astype(BF16).astype(F32)
    rest = v - high
    mid = rest.astype(BF16).astype(F32)
    return high, mid, (rest - mid).astype(BF16).astype(F32)


def pair_kernel(sq):
    inv = lax.rsqrt(sq)
    turns = sq * inv
    part = turns - jnp.round(turns)
    u = part * part
    half_sin = part * (3.14158208 + u * (-5.1671442 + u * (2.5419089 + u * -0.55465701)))
    half_cos = 0.9999933 + u * (-4.93393802 + u * (4.04128384 + u * -1.22212701))
    sine = half_sin * half_cos
    cosine = 0.5 - half_sin * half_sin
    z = inv * (1.0 / (2.0 * math.pi))
    a = inv * inv
    return (a * (sine + z * cosine)).astype(BF16), (a * (cosine - z * sine)).astype(BF16)


def body(
    pos_ref, ori_ref, area_ref, inc_ref, vis_ref, out_ref,
    st_obs, rx_obs, st_pw, rx_pw, st_vis, rx_vis, st_cur, rx_cur, st_sum, rx_sum,
    inc_pack, obs_all, pw_all, right_t, right, left, s_a, s_b, k_all, x_near, x_far, acc,
    send_sem, recv_sem,
):
    row, col = lax.axis_index("row"), lax.axis_index("col")
    x0, zl0 = lax.rem(row, NX), row // NX
    y0, zh0, c0 = col // 4, lax.rem(col // 2, 2), lax.rem(col, 2)
    z0 = zh0 * 4 + zl0

    def device(dx=0, dy=0, dz=0, dc=0):
        x, y, z, c = lax.rem(x0 + dx, NX), lax.rem(y0 + dy, NY), lax.rem(z0 + dz, NZ), lax.rem(c0 + dc, NC)
        return {"row": lax.rem(z, 4) * NX + x, "col": y * 4 + (z // 4) * 2 + c}

    barrier = pltpu.get_barrier_semaphore()
    for x, z in XZ:
        pl.semaphore_signal(barrier, inc=1, device_id=device(dx=x, dz=z), device_id_type=MESH)
    for y, c in YC:
        pl.semaphore_signal(barrier, inc=1, device_id=device(dy=y, dc=c), device_id_type=MESH)

    lane = lax.broadcasted_iota(jnp.int32, (8, 128), 1)
    sub = lax.broadcasted_iota(jnp.int32, (8, 128), 0)
    low = lane < TILE
    top = sub < 4

    def swap_halves(v):
        return pltpu.roll(v, TILE, axis=1)

    def wide(v):
        return jnp.concatenate([v, jnp.zeros((v.shape[0], 128 - v.shape[1]), v.dtype)], axis=1)

    pos = pos_ref[...]
    polar, azimuth = ori_ref[0:1, :], ori_ref[1:2, :]
    sin_p = jnp.sin(polar)
    st_obs[0] = jnp.zeros((8, 128), F32)
    st_obs[0, 0:3, 0:TILE] = pos
    st_obs[0, 3:4, 0:TILE] = sin_p * jnp.cos(azimuth)
    st_obs[0, 4:5, 0:TILE] = sin_p * jnp.sin(azimuth)
    st_obs[0, 5:6, 0:TILE] = jnp.cos(polar)
    st_obs[1] = swap_halves(st_obs[0])
    rx_obs[0] = st_obs[0]
    acc[0:8, 0:128] = jnp.zeros((8, 128), F32)
    acc[0:3, 0:TILE] = pos
    acc[3:4, 0:TILE] = area_ref[...] * (2.0 * 64.0 / math.sqrt(32768.0))
    own_pw = acc[0:8, 0:128]
    st_pw[0] = own_pw[0:4]
    st_pw[1] = swap_halves(own_pw)[0:4]
    rx_pw[0] = own_pw[0:4]
    st_vis[...] = jnp.concatenate([wide(vis_ref[b].astype(F32)) for b in range(16)], axis=0).astype(BF16)

    inc_pack[...] = jnp.zeros((8, 128), F32)
    for k in range(2):
        inc_pack[4 * k : 4 * k + 2, 0:TILE] = inc_ref[0, k]
        inc_pack[4 * k + 2 : 4 * k + 4, 0:TILE] = inc_ref[1, k]
    third = jnp.concatenate([inc_ref[0, 2], inc_ref[1, 2], jnp.zeros((4, TILE), F32)], axis=0)
    inc_pack[...] += swap_halves(wide(third))

    def stage_current(bounce, packed):
        st_cur[bounce, 0] = packed.astype(BF16)
        st_cur[bounce, 1] = swap_halves(packed).astype(BF16)
        rx_cur[bounce, 0] = st_cur[bounce, 0]

    stage_current(0, inc_pack[...])

    pl.semaphore_wait(barrier, len(XZ) + len(YC))

    def send(src, dst, sem, **offset):
        pltpu.make_async_remote_copy(
            src_ref=src, dst_ref=dst, send_sem=send_sem.at[sem], recv_sem=recv_sem.at[sem],
            device_id=device(**offset), device_id_type=MESH,
        ).start()

    def arrived(ref, sem):
        pltpu.make_async_copy(ref, ref, recv_sem.at[sem]).wait()

    def left_here(ref, sem):
        pltpu.make_async_copy(ref, ref, send_sem.at[sem]).wait()

    near_slots, far_slots = NEAR_Z * NX, (NZ - NEAR_Z) * NX
    S_OBS, S_VIS, S_PWN, S_PWF, S_CUR, S_SUM = 0, 1, 2, 3, 4, 10

    def sem_of(base, x, z):
        return base if src_slot(-x, -z) < near_slots else base + 1

    for x, z in XZ:
        send(st_pw.at[x % 2], rx_pw.at[src_slot(-x, -z)], sem_of(S_PWN, x, z), dx=x, dz=z)
    send(st_vis, rx_vis, S_VIS, dz=4)
    for y, c in YC:
        send(st_obs.at[c], rx_obs.at[(-y % NY) * NC + c], S_OBS, dy=y, dc=c)

    def send_current(bounce):
        for x, z in XZ:
            send(
                st_cur.at[bounce, x % 2], rx_cur.at[bounce, src_slot(-x, -z)],
                sem_of(S_CUR + 2 * bounce, x, z), dx=x, dz=z,
            )

    send_current(0)

    slot = lax.broadcasted_iota(jnp.int32, (32, 16), 0)
    there = lax.broadcasted_iota(jnp.int32, (32, 16), 1)
    place = slot // NX
    z_off = jnp.where(lax.rem(place, 2) == 1, (place + 1) // 2, lax.rem(NZ - place // 2, NZ))
    z_of = lax.rem(z0 + z_off, NZ)
    match = there == lax.rem(z_of, 4) * NX + lax.rem(x0 + lax.rem(slot, NX), NX)
    own_z = (z_of // 4) == zh0
    pick_own = jnp.where(match & own_z, 1.0, 0.0).astype(BF16)
    pick_far = jnp.where(match & jnp.logical_not(own_z), 1.0, 0.0).astype(BF16)
    a_row = lax.broadcasted_iota(jnp.int32, (128, NOBS), 0)
    a_lane = lax.broadcasted_iota(jnp.int32, (128, NOBS), 1)
    a_of = (
        lax.rem(y0 + a_lane // 128, NY) * 4 + zh0 * 2 + lax.rem(c0 + lax.rem(a_lane // TILE, 2), 2)
    )
    spread = jnp.where(a_row == a_of, 1.0, 0.0).astype(BF16)

    right_t[...] = jnp.zeros((128, NSRC), F32)
    right_t[18:24, :] = jnp.ones((6, NSRC), F32)
    b_row = lax.broadcasted_iota(jnp.int32, (32, NSRC), 0)
    b_lane = lax.broadcasted_iota(jnp.int32, (32, NSRC), 1)
    right_t[24:56, :] = jnp.where(b_row == b_lane // TILE, 1.0, 0.0)

    arrived(rx_obs.at[pl.ds(1, NY * NC - 1)], S_OBS)
    for y in range(NY):
        obs_all[:, y * 128 : (y + 1) * 128] = rx_obs[2 * y] + rx_obs[2 * y + 1]
    big_pos = 4.0 * obs_all[0:3, :]
    h, m, l = split3(big_pos)
    for i, part in enumerate((h, m, l, h, m, h)):
        left[3 * i : 3 * i + 3, :] = part
    left[18:21, :] = jnp.ones((3, NOBS), F32)
    norms = split3(jnp.sum(big_pos * big_pos, axis=0, keepdims=True) + 16.0 * 0.0025)
    for i, part in enumerate(norms):
        left[21 + i : 22 + i, :] = part
    arrived(rx_vis, S_VIS)
    seen = jnp.dot(pick_own, st_vis[...], preferred_element_type=F32) + jnp.dot(
        pick_far, rx_vis[...], preferred_element_type=F32
    )
    seen_all = jnp.dot(seen.astype(BF16), spread, preferred_element_type=F32)
    left[24:56, :] = BIG * (1.0 - seen_all)
    left[56:64, :] = jnp.zeros((8, NOBS), F32)

    arrived(rx_pw.at[pl.ds(1, near_slots - 1)], S_PWN)
    arrived(rx_pw.at[pl.ds(near_slots, far_slots)], S_PWF)
    for g in range(NSRC // 128):
        pw_all[:, g * 128 : (g + 1) * 128] = rx_pw[2 * g] + rx_pw[2 * g + 1]
    big_src = 4.0 * pw_all[0:3, :]
    h, m, l = split3(big_src)
    for i, part in enumerate((h, h, h, m, m, l)):
        right_t[3 * i : 3 * i + 3, :] = -2.0 * part
    norms = split3(jnp.sum(big_src * big_src, axis=0, keepdims=True))
    for i, part in enumerate(norms):
        right_t[18 + i : 19 + i, :] = part
    for g in range(NSRC // 128):
        right[g * 128 : (g + 1) * 128, :] = jnp.transpose(right_t[:, g * 128 : (g + 1) * 128]).astype(BF16)

    def operand(bounce, groups, first, x_ref):
        span = len(groups) * 128
        for g in groups:
            lanes = slice(g * 128, (g + 1) * 128)
            even, odd = rx_cur[bounce, 2 * g].astype(F32), rx_cur[bounce, 2 * g + 1].astype(F32)
            same = jnp.where(low, even, odd)
            s = (same, pltpu.roll(same, 4, axis=0), swap_halves(jnp.where(low, odd, even)))
            p = [pw_all[k : k + 1, lanes] for k in range(3)]
            w = pw_all[3:4, lanes]
            rows = []
            turned = []
            for k in range(3):
                i, j = (k + 1) % 3, (k + 2) % 3
                cross = p[i] * s[j] - p[j] * s[i]
                both = jnp.where(top, s[k], pltpu.roll(cross, 4, axis=0)) * w
                rows.append(both)
                turned.append(
                    jnp.where(lax.rem(sub, 4) < 2, -pltpu.roll(both, 6, axis=0), pltpu.roll(both, 2, axis=0))
                )
            at = (g - first) * 128
            x_ref[:, at : at + 128] = jnp.concatenate(rows, axis=0).astype(BF16)
            x_ref[:, span + at : span + at + 128] = jnp.concatenate(turned, axis=0).astype(BF16)

    near_groups = range(0, NEAR // 128)
    far_groups = range(NEAR // 128, NSRC // 128)

    def near_operand(bounce):
        arrived(rx_cur.at[bounce, pl.ds(1, near_slots - 1)], S_CUR + 2 * bounce)
        operand(bounce, near_groups, 0, x_near)

    def far_operand(bounce):
        arrived(rx_cur.at[bounce, pl.ds(near_slots, far_slots)], S_CUR + 2 * bounce + 1)
        operand(bounce, far_groups, NEAR // 128, x_far)

    def near_product(lanes):
        return jnp.dot(x_near[...], k_all[0 : 2 * NEAR, lanes], preferred_element_type=F32)

    def far_product(lanes):
        return jnp.dot(x_far[...], k_all[2 * NEAR : 2 * NSRC, lanes], preferred_element_type=F32)

    def messages(bounce, y, total):
        lanes = slice(y * 128, (y + 1) * 128)
        p = [obs_all[k : k + 1, lanes] for k in range(3)]
        n = [obs_all[3 + k : 4 + k, lanes] for k in range(3)]
        a = [total[8 * k : 8 * k + 8, :] for k in range(3)]
        d = [
            p[(k + 1) % 3] * a[(k + 2) % 3] - p[(k + 2) % 3] * a[(k + 1) % 3] - pltpu.roll(a[k], 4, axis=0)
            for k in range(3)
        ]
        s = [n[(k + 1) % 3] * d[(k + 2) % 3] - n[(k + 2) % 3] * d[(k + 1) % 3] for k in range(3)]
        pair = jnp.where(top, s[0], pltpu.roll(s[1], 4, axis=0))
        for c, packed in (
            (0, jnp.where(low, pair, swap_halves(s[2]))),
            (1, jnp.where(low, swap_halves(pair), s[2])),
        ):
            if y == 0 and c == 0:
                rx_sum[bounce, 0] = packed.astype(BF16)
            else:
                st_sum[bounce, 2 * y + c] = packed.astype(BF16)
                send(
                    st_sum.at[bounce, 2 * y + c], rx_sum.at[bounce, (-y % NY) * NC + c],
                    S_SUM + bounce, dy=y, dc=c,
                )

    blocks = NSRC // BLOCK
    steps = (NOBS // BLOCK) * blocks

    def squares(step, ref):
        step = lax.rem(step, steps)
        rows = pl.ds(pl.multiple_of(lax.rem(step, blocks) * BLOCK, BLOCK), BLOCK)
        lanes = pl.ds(pl.multiple_of((step // blocks) * BLOCK, BLOCK), BLOCK)
        ref[...] = jnp.dot(
            right[rows, 0:DEPTH], left[:, lanes].astype(BF16), preferred_element_type=F32
        )

    def fill(ref, block, q):
        re_row = pl.multiple_of(block * BLOCK + jnp.where(block < NEAR // BLOCK, 0, NEAR), BLOCK)
        im_row = pl.multiple_of(block * BLOCK + jnp.where(block < NEAR // BLOCK, NEAR, NSRC), BLOCK)
        for r in range(0, BLOCK, 64):
            for v in range(0, BLOCK, 128):
                re, im = pair_kernel(ref[r : r + 64, v : v + 128])
                k_all[pl.ds(re_row + r, 64), q * BLOCK + v : q * BLOCK + v + 128] = re
                k_all[pl.ds(im_row + r, 64), q * BLOCK + v : q * BLOCK + v + 128] = im

    quarters = (2, 1, 3, 0)
    near_operand(0)
    far_operand(0)
    squares(jnp.int32(quarters[0] * blocks), s_a)
    for n, q in enumerate(quarters):
        after = quarters[(n + 1) % len(quarters)]

        def two(i, _, q=q, after=after):
            squares(q * blocks + 2 * i + 1, s_b)
            fill(s_a, 2 * i, q)
            squares(jnp.where(2 * i + 2 < blocks, q * blocks + 2 * i + 2, after * blocks), s_a)
            fill(s_b, 2 * i + 1, q)
            return 0

        lax.fori_loop(0, blocks // 2, two, 0)
        lanes = slice(q * BLOCK, (q + 1) * BLOCK)
        total = near_product(lanes) + far_product(lanes)
        for y in (2 * q + 1, 2 * q):
            messages(0, y, total[:, (y % 2) * 128 : (y % 2) * 128 + 128])

    current = None
    for bounce in range(ITERS):
        if bounce > 0:
            near_operand(bounce)
            for q in quarters:
                lanes = slice(q * BLOCK, (q + 1) * BLOCK)
                acc[:, lanes] = near_product(lanes)
            far_operand(bounce)
            for q in quarters:
                lanes = slice(q * BLOCK, (q + 1) * BLOCK)
                total = acc[:, lanes] + far_product(lanes)
                for y in (2 * q + 1, 2 * q):
                    messages(bounce, y, total[:, (y % 2) * 128 : (y % 2) * 128 + 128])
        arrived(rx_sum.at[bounce, pl.ds(1, NY * NC - 1)], S_SUM + bounce)
        current = inc_pack[...] + jnp.sum(rx_sum[bounce].astype(F32), axis=0)
        if bounce + 1 < ITERS:
            stage_current(bounce + 1, current)
            send_current(bounce + 1)

    third = swap_halves(current)
    for part in range(2):
        for k in range(2):
            out_ref[part, k] = current[4 * k + 2 * part : 4 * k + 2 * part + 2, 0:TILE]
        out_ref[part, 2] = third[2 * part : 2 * part + 2, 0:TILE]

    left_here(rx_obs.at[pl.ds(1, NY * NC - 1)], S_OBS)
    left_here(rx_vis, S_VIS)
    left_here(rx_pw.at[pl.ds(1, near_slots - 1)], S_PWN)
    left_here(rx_pw.at[pl.ds(near_slots, far_slots)], S_PWF)
    for bounce in range(ITERS):
        left_here(rx_cur.at[bounce, pl.ds(1, near_slots - 1)], S_CUR + 2 * bounce)
        left_here(rx_cur.at[bounce, pl.ds(near_slots, far_slots)], S_CUR + 2 * bounce + 1)
        left_here(rx_sum.at[bounce, pl.ds(1, NY * NC - 1)], S_SUM + bounce)


def shards(positions, orient, areas, incident, visible):
    vmem = pltpu.VMEM
    scratch = [
        vmem((2, 8, 128), F32), vmem((16, 8, 128), F32),
        vmem((2, 4, 128), F32), vmem((32, 4, 128), F32),
        vmem((16, 128), BF16), vmem((16, 128), BF16),
        vmem((ITERS, 2, 8, 128), BF16), vmem((ITERS, 32, 8, 128), BF16),
        vmem((ITERS, 16, 8, 128), BF16), vmem((ITERS, 16, 8, 128), BF16),
        vmem((8, 128), F32), vmem((8, NOBS), F32), vmem((4, NSRC), F32),
        vmem((128, NSRC), F32), vmem((NSRC, 128), BF16), vmem((DEPTH, NOBS), F32),
        vmem((BLOCK, BLOCK), F32), vmem((BLOCK, BLOCK), F32),
        vmem((2 * NSRC, NOBS), BF16),
        vmem((24, 2 * NEAR), BF16), vmem((24, 2 * FAR), BF16), vmem((24, NOBS), F32),
        pltpu.SemaphoreType.DMA((13,)), pltpu.SemaphoreType.DMA((13,)),
    ]
    return pl.pallas_call(
        body,
        out_shape=jax.ShapeDtypeStruct(incident.shape, F32),
        in_specs=[pl.BlockSpec(memory_space=vmem)] * 5,
        out_specs=pl.BlockSpec(memory_space=vmem),
        scratch_shapes=scratch,
        compiler_params=pltpu.CompilerParams(
            collective_id=0, has_side_effects=True, vmem_limit_bytes=48 * 2**20
        ),
        cost_estimate=pl.CostEstimate(flops=3_000_000_000, bytes_accessed=1_000_000, transcendentals=4_000_000),
    )(positions, orient, areas.reshape(1, -1), incident, jnp.transpose(visible, (1, 2, 0)))


def solution(mesh):
    in_specs = (
        P(None, ("row", "col")),
        P(None, ("row", "col")),
        P(("row", "col")),
        P(None, None, None, ("row", "col")),
        P("row", None, "col"),
    )
    out_specs = P(None, None, None, ("row", "col"))
    return jax.shard_map(shards, mesh=mesh, in_specs=in_specs, out_specs=out_specs, check_vma=False)
```

```python
import math

import jax
import jax.numpy as jnp
from jax import lax
from jax.experimental import pallas as pl
from jax.experimental.pallas import tpu as pltpu
from jax.sharding import PartitionSpec as P

ITERS = 3
TILE = 64
MESH = pl.DeviceIdType.MESH
F32, BF16 = jnp.float32, jnp.bfloat16

NX, NY, NZ, NC = 4, 8, 8, 2
RING_ORDER = (0, 1, 7, 2, 6, 3, 5, 4)
NEAR_Z = 5
NOBS = NY * NC * TILE
NSRC = NX * NZ * TILE
NEAR = NEAR_Z * NX * TILE
FAR = NSRC - NEAR
DEPTH = 64
BLOCK = 256
HALF = NOBS // 2
ROWS = 48
BIG = 2.0**127

YC = tuple((y, c) for y in (4, 3, 5, 2, 6, 1, 7, 0) for c in (1, 0) if y or c)
XZ = tuple(
    (x, z)
    for x, z in sorted(
        ((x, z) for x in range(NX) for z in range(NZ) if x or z),
        key=lambda p: -(min(p[0], NX - p[0]) + min(p[1], NZ - p[1])),
    )
)


def src_slot(x, z):
    return RING_ORDER.index(z % NZ) * NX + x % NX


def obs_slot(y, c):
    return RING_ORDER.index(y % NY) * NC + c % NC


def ring_offset(place):
    return jnp.where(lax.rem(place, 2) == 1, (place + 1) // 2, lax.rem(8 - place // 2, 8))


def aligned(v, n):
    return v if isinstance(v, int) else pl.multiple_of(v, n)


def either(which, a, b):
    return (a if which else b) if isinstance(which, bool) else jnp.where(which, a, b)


def split3(v):
    high = v.astype(BF16).astype(F32)
    rest = v - high
    mid = rest.astype(BF16).astype(F32)
    return high, mid, (rest - mid).astype(BF16).astype(F32)


def pair_kernel(sq):
    inv = lax.rsqrt(sq)
    halves = sq * inv
    whole = jnp.round(halves)
    part = (halves - whole).astype(BF16)
    count = whole.astype(BF16)
    odd = count - ((count + BF16(384.0)) - BF16(384.0))
    a = (inv * inv).astype(BF16) * (BF16(1.0) - BF16(2.0) * (odd * odd))
    z = inv.astype(BF16) * BF16(1.0 / math.pi)
    u = part * part
    sine = part * (BF16(3.14064334) + u * (BF16(-5.13694906) + u * BF16(2.29967451)))
    cosine = BF16(0.99940325) + u * (BF16(-4.89118702) + u * BF16(3.58384395))
    return a * (sine + z * cosine), a * (cosine - z * sine)


def body(
    pos_hbm, ori_hbm, area_hbm, inc_hbm, vis_hbm, out_ref,
    pos_ref, ori_ref, area_ref, inc_ref, vis_ref, st_obs, rx_obs, st_pw, rx_pw, st_vis, rx_vis, st_cur, rx_cur, st_sum, rx_sum,
    inc_pack, obs_all, pw_all, right_t, right, left_f, left, s_a, s_b, k_all, x_near, x_far, acc,
    load_sem, send_sem, recv_sem,
):
    row, col = lax.axis_index("row"), lax.axis_index("col")
    x0, zl0 = lax.rem(row, NX), row // NX
    y0, zh0, c0 = col // 4, lax.rem(col // 2, 2), lax.rem(col, 2)
    z0 = zh0 * 4 + zl0

    def device(dx=0, dy=0, dz=0, dc=0):
        x, y, z, c = lax.rem(x0 + dx, NX), lax.rem(y0 + dy, NY), lax.rem(z0 + dz, NZ), lax.rem(c0 + dc, NC)
        return {"row": lax.rem(z, 4) * NX + x, "col": y * 4 + (z // 4) * 2 + c}

    loads = [
        pltpu.make_async_copy(src, dst, load_sem.at[i])
        for i, (src, dst) in enumerate(
            ((pos_hbm, pos_ref), (ori_hbm, ori_ref), (area_hbm, area_ref), (vis_hbm, vis_ref), (inc_hbm, inc_ref))
        )
    ]
    for load in loads:
        load.start()
    barrier = pltpu.get_barrier_semaphore()
    for x, z in XZ:
        pl.semaphore_signal(barrier, inc=1, device_id=device(dx=x, dz=z), device_id_type=MESH)
    for y, c in YC:
        pl.semaphore_signal(barrier, inc=1, device_id=device(dy=y, dc=c), device_id_type=MESH)

    lane = lax.broadcasted_iota(jnp.int32, (8, 128), 1)
    sub = lax.broadcasted_iota(jnp.int32, (8, 128), 0)
    low = lane < TILE
    top = sub < 4

    def swap_halves(v):
        return pltpu.roll(v, TILE, axis=1)

    def wide(v):
        return jnp.concatenate([v, jnp.zeros((v.shape[0], 128 - v.shape[1]), v.dtype)], axis=1)

    for load in loads:
        load.wait()

    pos = pos_ref[...]
    polar, azimuth = ori_ref[0:1, :], ori_ref[1:2, :]
    sin_p = jnp.sin(polar)
    st_obs[0] = jnp.zeros((8, 128), F32)
    st_obs[0, 0:3, 0:TILE] = pos
    st_obs[0, 3:4, 0:TILE] = sin_p * jnp.cos(azimuth)
    st_obs[0, 4:5, 0:TILE] = sin_p * jnp.sin(azimuth)
    st_obs[0, 5:6, 0:TILE] = jnp.cos(polar)
    st_obs[1] = swap_halves(st_obs[0])
    rx_obs[0] = st_obs[0]
    acc[0:8, 0:128] = jnp.zeros((8, 128), F32)
    acc[0:3, 0:TILE] = pos
    acc[3:4, 0:TILE] = area_ref[...] * (2.0 * 128.0 / math.sqrt(32768.0))
    own_pw = acc[0:8, 0:128]
    st_pw[0] = own_pw[0:4]
    st_pw[1] = swap_halves(own_pw)[0:4]
    rx_pw[0] = own_pw[0:4]
    st_vis[...] = jnp.concatenate([wide(vis_ref[b].astype(F32)) for b in range(16)], axis=0).astype(BF16)

    inc_pack[...] = jnp.zeros((8, 128), F32)
    for k in range(2):
        inc_pack[4 * k : 4 * k + 2, 0:TILE] = inc_ref[0, k]
        inc_pack[4 * k + 2 : 4 * k + 4, 0:TILE] = inc_ref[1, k]
    third = jnp.concatenate([inc_ref[0, 2], inc_ref[1, 2], jnp.zeros((4, TILE), F32)], axis=0)
    inc_pack[...] += swap_halves(wide(third))

    def stage_current(bounce, packed):
        st_cur[bounce, 0] = packed.astype(BF16)
        st_cur[bounce, 1] = swap_halves(packed).astype(BF16)
        rx_cur[bounce, 0] = st_cur[bounce, 0]

    stage_current(0, inc_pack[...])

    slot = lax.broadcasted_iota(jnp.int32, (32, 16), 0)
    there = lax.broadcasted_iota(jnp.int32, (32, 16), 1)
    place = slot // NX
    z_of = lax.rem(z0 + ring_offset(place), NZ)
    match = there == lax.rem(z_of, 4) * NX + lax.rem(x0 + lax.rem(slot, NX), NX)
    own_z = (z_of // 4) == zh0
    pick_own = jnp.where(match & own_z, 1.0, 0.0).astype(BF16)
    pick_far = jnp.where(match & jnp.logical_not(own_z), 1.0, 0.0).astype(BF16)
    a_row = lax.broadcasted_iota(jnp.int32, (128, NOBS), 0)
    a_lane = lax.broadcasted_iota(jnp.int32, (128, NOBS), 1)
    a_of = (
        lax.rem(y0 + ring_offset(a_lane // 128), NY) * 4 + zh0 * 2 + lax.rem(c0 + lax.rem(a_lane // TILE, 2), 2)
    )
    spread = jnp.where(a_row == a_of, 1.0, 0.0).astype(BF16)

    right_t[...] = jnp.zeros((DEPTH, NSRC), F32)
    right_t[18:24, :] = jnp.ones((6, NSRC), F32)
    b_row = lax.broadcasted_iota(jnp.int32, (32, NSRC), 0)
    b_lane = lax.broadcasted_iota(jnp.int32, (32, NSRC), 1)
    right_t[24:56, :] = jnp.where(b_row == b_lane // TILE, 1.0, 0.0)

    pl.semaphore_wait(barrier, len(XZ) + len(YC))

    def send(src, dst, sem, **offset):
        pltpu.make_async_remote_copy(
            src_ref=src, dst_ref=dst, send_sem=send_sem.at[sem], recv_sem=recv_sem.at[sem],
            device_id=device(**offset), device_id_type=MESH,
        ).start()

    def arrived(ref, sem):
        pltpu.make_async_copy(ref, ref, recv_sem.at[sem]).wait()

    def left_here(ref, sem):
        pltpu.make_async_copy(ref, ref, send_sem.at[sem]).wait()

    near_slots, far_slots = NEAR_Z * NX, (NZ - NEAR_Z) * NX
    S_OBS, S_VIS, S_PWN, S_PWF, S_CUR, S_SUM = 0, 1, 2, 3, 4, 10

    def sem_of(base, x, z):
        return base if src_slot(-x, -z) < near_slots else base + 1

    def send_place(near):
        for x, z in XZ:
            if (src_slot(-x, -z) < near_slots) == near:
                send(st_pw.at[x % 2], rx_pw.at[src_slot(-x, -z)], sem_of(S_PWN, x, z), dx=x, dz=z)

    send(st_vis, rx_vis, S_VIS, dz=4)
    for y, c in YC:
        send(st_obs.at[c], rx_obs.at[obs_slot(-y, c)], S_OBS, dy=y, dc=c)
    send_place(True)
    send_place(False)

    def send_current(bounce):
        for x, z in XZ:
            send(
                st_cur.at[bounce, x % 2], rx_cur.at[bounce, src_slot(-x, -z)],
                sem_of(S_CUR + 2 * bounce, x, z), dx=x, dz=z,
            )

    send_current(0)

    arrived(rx_obs.at[pl.ds(1, NY * NC - 1)], S_OBS)
    for y in range(NY):
        obs_all[:, y * 128 : (y + 1) * 128] = rx_obs[2 * y] + rx_obs[2 * y + 1]
    big_pos = 8.0 * obs_all[0:3, :]
    h, m, l = split3(big_pos)
    for i, part in enumerate((h, m, l, h, m, h)):
        left_f[3 * i : 3 * i + 3, :] = part
    left_f[18:21, :] = jnp.ones((3, NOBS), F32)
    norms = split3(jnp.sum(big_pos * big_pos, axis=0, keepdims=True) + 64.0 * 0.0025)
    for i, part in enumerate(norms):
        left_f[21 + i : 22 + i, :] = part
    left_f[56:64, :] = jnp.zeros((8, NOBS), F32)

    def source_side(first, count):
        groups = range(first // 128, (first + count) // 128)
        for g in groups:
            pw_all[:, g * 128 : (g + 1) * 128] = rx_pw[2 * g] + rx_pw[2 * g + 1]
        span = slice(first, first + count)
        big_src = 8.0 * pw_all[0:3, span]
        h, m, l = split3(big_src)
        for i, part in enumerate((h, h, h, m, m, l)):
            right_t[3 * i : 3 * i + 3, span] = -2.0 * part
        norms = split3(jnp.sum(big_src * big_src, axis=0, keepdims=True))
        for i, part in enumerate(norms):
            right_t[18 + i : 19 + i, span] = part
        for g in groups:
            right[g * 128 : (g + 1) * 128, :] = jnp.transpose(right_t[:, g * 128 : (g + 1) * 128]).astype(BF16)

    arrived(rx_pw.at[pl.ds(1, near_slots - 1)], S_PWN)
    source_side(0, NEAR)
    arrived(rx_vis, S_VIS)
    seen = jnp.dot(pick_own, st_vis[...], preferred_element_type=F32) + jnp.dot(
        pick_far, rx_vis[...], preferred_element_type=F32
    )
    seen_all = jnp.dot(seen.astype(BF16), spread, preferred_element_type=F32)
    left_f[24:56, :] = BIG * (1.0 - seen_all)
    left[...] = left_f[...].astype(BF16)

    def operand(bounce, groups, first, x_ref):
        span = len(groups) * 128
        for g in groups:
            lanes = slice(g * 128, (g + 1) * 128)
            even, odd = rx_cur[bounce, 2 * g].astype(F32), rx_cur[bounce, 2 * g + 1].astype(F32)
            same = jnp.where(low, even, odd)
            s = (same, pltpu.roll(same, 4, axis=0), swap_halves(jnp.where(low, odd, even)))
            p = [pw_all[k : k + 1, lanes] for k in range(3)]
            w = pw_all[3:4, lanes]
            rows = []
            turned = []
            for k in range(3):
                i, j = (k + 1) % 3, (k + 2) % 3
                cross = p[i] * s[j] - p[j] * s[i]
                both = jnp.where(top, s[k], pltpu.roll(cross, 4, axis=0)) * w
                rows.append(both)
                turned.append(
                    jnp.where(lax.rem(sub, 4) < 2, -pltpu.roll(both, 6, axis=0), pltpu.roll(both, 2, axis=0))
                )
            at = (g - first) * 128
            for begin, parts in ((at, rows), (span + at, turned)):
                exact = jnp.concatenate(parts, axis=0)
                high = exact.astype(BF16)
                rest = (exact - high.astype(F32)).astype(BF16)
                x_ref[:, begin : begin + 128] = jnp.concatenate([high, rest], axis=0)

    near_groups = range(0, NEAR // 128)
    far_groups = range(NEAR // 128, NSRC // 128)

    def near_operand(bounce):
        arrived(rx_cur.at[bounce, pl.ds(1, near_slots - 1)], S_CUR + 2 * bounce)
        operand(bounce, near_groups, 0, x_near)

    def far_operand(bounce):
        arrived(rx_cur.at[bounce, pl.ds(near_slots, far_slots)], S_CUR + 2 * bounce + 1)
        operand(bounce, far_groups, NEAR // 128, x_far)

    def near_product(lanes):
        both = jnp.dot(x_near[...], k_all[0 : 2 * NEAR, lanes], preferred_element_type=F32)
        return both[0 : ROWS // 2] + both[ROWS // 2 : ROWS]

    def far_product(lanes):
        both = jnp.dot(x_far[...], k_all[2 * NEAR : 2 * NSRC, lanes], preferred_element_type=F32)
        return both[0 : ROWS // 2] + both[ROWS // 2 : ROWS]

    def messages(bounce, place, total):
        lanes = slice(place * 128, (place + 1) * 128)
        y = RING_ORDER[place]
        p = [obs_all[k : k + 1, lanes] for k in range(3)]
        n = [obs_all[3 + k : 4 + k, lanes] for k in range(3)]
        a = [total[8 * k : 8 * k + 8, :] for k in range(3)]
        d = [
            p[(k + 1) % 3] * a[(k + 2) % 3] - p[(k + 2) % 3] * a[(k + 1) % 3] - pltpu.roll(a[k], 4, axis=0)
            for k in range(3)
        ]
        s = [n[(k + 1) % 3] * d[(k + 2) % 3] - n[(k + 2) % 3] * d[(k + 1) % 3] for k in range(3)]
        pair = jnp.where(top, s[0], pltpu.roll(s[1], 4, axis=0))
        for c, packed in (
            (0, jnp.where(low, pair, swap_halves(s[2]))),
            (1, jnp.where(low, swap_halves(pair), s[2])),
        ):
            if place == 0 and c == 0:
                rx_sum[bounce, 0] = packed.astype(BF16)
            else:
                st_sum[bounce, 2 * place + c] = packed.astype(BF16)
                send(
                    st_sum.at[bounce, 2 * place + c], rx_sum.at[bounce, obs_slot(-y, c)],
                    S_SUM + bounce, dy=y, dc=c,
                )

    def squares(block, lanes, ref):
        rows = pl.ds(aligned(block * BLOCK, BLOCK), BLOCK)
        ref[:, 0 : lanes.size] = jnp.dot(right[rows, :], left[:, lanes], preferred_element_type=F32)

    def fill(ref, block, lanes):
        near = block < NEAR // BLOCK
        re_row = aligned(block * BLOCK + either(near, 0, NEAR), BLOCK)
        im_row = aligned(block * BLOCK + either(near, NEAR, NSRC), BLOCK)
        for r in range(0, BLOCK, 16):
            for v in range(0, lanes.size, 256):
                re, im = pair_kernel(ref[r : r + 16, v : v + 256])
                at = pl.ds(aligned(lanes.start + v, BLOCK), BLOCK)
                k_all[pl.ds(re_row + r, 16), at] = re
                k_all[pl.ds(im_row + r, 16), at] = im

    def sweep(unit, count, last):
        squares(*unit(0), s_a)

        def two(i, _):
            squares(*unit(2 * i + 1), s_b)
            fill(s_a, *unit(2 * i))
            squares(*unit(jnp.minimum(2 * i + 2, last)), s_a)
            fill(s_b, *unit(2 * i + 1))
            return 0

        lax.fori_loop(0, count // 2, two, 0)

    near_blocks, far_blocks = NEAR // BLOCK, FAR // BLOCK
    sweep(
        lambda k: (k // 2, pl.ds(pl.multiple_of(lax.rem(k, 2) * HALF, HALF), HALF)),
        2 * near_blocks, 2 * near_blocks - 1,
    )
    near_operand(0)
    arrived(rx_pw.at[pl.ds(near_slots, far_slots)], S_PWF)
    source_side(NEAR, FAR)
    far_operand(0)

    def finish(bounce, q):
        lanes = slice(q * BLOCK, (q + 1) * BLOCK)
        total = acc[:, lanes] + far_product(lanes)
        for place in (2 * q + 1, 2 * q):
            messages(bounce, place, total[:, (place % 2) * 128 : (place % 2) * 128 + 128])

    for h in (1, 0):
        units = [
            (near_blocks + b, pl.ds(h * HALF + q * BLOCK, BLOCK)) for q in (1, 0) for b in range(far_blocks)
        ]
        stages = (s_a, s_b)
        squares(*units[0], s_a)
        for k, unit in enumerate(units):
            if k + 1 < len(units):
                squares(*units[k + 1], stages[(k + 1) % 2])
            if k % far_blocks == 0:
                q = 2 * h + 1 - k // far_blocks
                acc[:, q * BLOCK : (q + 1) * BLOCK] = near_product(slice(q * BLOCK, (q + 1) * BLOCK))
            fill(stages[k % 2], *unit)
            if k % far_blocks == far_blocks - 1:
                finish(0, 2 * h + 1 - k // far_blocks)

    current = None
    for bounce in range(ITERS):
        if bounce > 0:
            near_operand(bounce)
            for h in (1, 0):
                acc[:, h * HALF : (h + 1) * HALF] = near_product(slice(h * HALF, (h + 1) * HALF))
            far_operand(bounce)
            for q in (3, 2, 1, 0):
                finish(bounce, q)
        arrived(rx_sum.at[bounce, pl.ds(1, NY * NC - 1)], S_SUM + bounce)
        current = inc_pack[...] + jnp.sum(rx_sum[bounce].astype(F32), axis=0)
        if bounce + 1 < ITERS:
            stage_current(bounce + 1, current)
            send_current(bounce + 1)

    third = swap_halves(current)
    for part in range(2):
        for k in range(2):
            out_ref[part, k] = current[4 * k + 2 * part : 4 * k + 2 * part + 2, 0:TILE]
        out_ref[part, 2] = third[2 * part : 2 * part + 2, 0:TILE]

    left_here(rx_obs.at[pl.ds(1, NY * NC - 1)], S_OBS)
    left_here(rx_vis, S_VIS)
    left_here(rx_pw.at[pl.ds(1, near_slots - 1)], S_PWN)
    left_here(rx_pw.at[pl.ds(near_slots, far_slots)], S_PWF)
    for bounce in range(ITERS):
        left_here(rx_cur.at[bounce, pl.ds(1, near_slots - 1)], S_CUR + 2 * bounce)
        left_here(rx_cur.at[bounce, pl.ds(near_slots, far_slots)], S_CUR + 2 * bounce + 1)
        left_here(rx_sum.at[bounce, pl.ds(1, NY * NC - 1)], S_SUM + bounce)


def shards(positions, orient, areas, incident, visible):
    vmem = pltpu.VMEM
    scratch = [
        vmem((3, TILE), F32), vmem((2, TILE), F32), vmem((1, TILE), F32), vmem(incident.shape, F32),
        vmem((16, 1, 32), jnp.int32),
        vmem((2, 8, 128), F32), vmem((16, 8, 128), F32),
        vmem((2, 4, 128), F32), vmem((32, 4, 128), F32),
        vmem((16, 128), BF16), vmem((16, 128), BF16),
        vmem((ITERS, 2, 8, 128), BF16), vmem((ITERS, 32, 8, 128), BF16),
        vmem((ITERS, 16, 8, 128), BF16), vmem((ITERS, 16, 8, 128), BF16),
        vmem((8, 128), F32), vmem((8, NOBS), F32), vmem((4, NSRC), F32),
        vmem((DEPTH, NSRC), F32), vmem((NSRC, DEPTH), BF16), vmem((DEPTH, NOBS), F32), vmem((DEPTH, NOBS), BF16),
        vmem((BLOCK, HALF), F32), vmem((BLOCK, HALF), F32),
        vmem((2 * NSRC, NOBS), BF16),
        vmem((ROWS, 2 * NEAR), BF16), vmem((ROWS, 2 * FAR), BF16), vmem((ROWS // 2, NOBS), F32),
        pltpu.SemaphoreType.DMA((5,)), pltpu.SemaphoreType.DMA((13,)), pltpu.SemaphoreType.DMA((13,)),
    ]
    return pl.pallas_call(
        body,
        out_shape=jax.ShapeDtypeStruct(incident.shape, F32),
        in_specs=[pl.BlockSpec(memory_space=pl.ANY)] * 5,
        out_specs=pl.BlockSpec(memory_space=vmem),
        scratch_shapes=scratch,
        compiler_params=pltpu.CompilerParams(
            collective_id=0, has_side_effects=True, vmem_limit_bytes=60 * 2**20
        ),
        cost_estimate=pl.CostEstimate(flops=3_000_000_000, bytes_accessed=1_000_000, transcendentals=4_000_000),
    )(positions, orient, areas.reshape(1, -1), incident, jnp.transpose(visible, (1, 2, 0)))


def solution(mesh):
    in_specs = (
        P(None, ("row", "col")),
        P(None, ("row", "col")),
        P(("row", "col")),
        P(None, None, None, ("row", "col")),
        P("row", None, "col"),
    )
    out_specs = P(None, None, None, ("row", "col"))
    return jax.shard_map(shards, mesh=mesh, in_specs=in_specs, out_specs=out_specs, check_vma=False)
```

```python
import math

import jax
import jax.numpy as jnp
from jax import lax
from jax.experimental import pallas as pl
from jax.experimental.pallas import tpu as pltpu
from jax.sharding import PartitionSpec as P

ITERS = 3
TILE = 64
MESH = pl.DeviceIdType.MESH
F32, BF16 = jnp.float32, jnp.bfloat16

NX, NY, NZ, NC = 4, 8, 8, 2
RING_ORDER = (0, 1, 7, 2, 6, 3, 5, 4)
NEAR_Z = 5
NOBS = NY * NC * TILE
NSRC = NX * NZ * TILE
NEAR = NEAR_Z * NX * TILE
FAR = NSRC - NEAR
DEPTH = 64
BLOCK = 256
HALF = NOBS // 2
ROWS = 48
BIG = 2.0**127

YC = tuple((y, c) for y in (4, 3, 5, 2, 6, 1, 7, 0) for c in (1, 0) if y or c)
XZ = tuple(
    (x, z)
    for x, z in sorted(
        ((x, z) for x in range(NX) for z in range(NZ) if x or z),
        key=lambda p: -(min(p[0], NX - p[0]) + min(p[1], NZ - p[1])),
    )
)


def src_slot(x, z):
    return RING_ORDER.index(z % NZ) * NX + x % NX


def obs_slot(y, c):
    return RING_ORDER.index(y % NY) * NC + c % NC


def ring_offset(place):
    return jnp.where(lax.rem(place, 2) == 1, (place + 1) // 2, lax.rem(8 - place // 2, 8))


def aligned(v, n):
    return v if isinstance(v, int) else pl.multiple_of(v, n)


def either(which, a, b):
    return (a if which else b) if isinstance(which, bool) else jnp.where(which, a, b)


def split3(v):
    high = v.astype(BF16).astype(F32)
    rest = v - high
    mid = rest.astype(BF16).astype(F32)
    return high, mid, (rest - mid).astype(BF16).astype(F32)


def pair_kernel(sq):
    inv = lax.rsqrt(sq)
    halves = sq * inv
    whole = jnp.round(halves)
    part = (halves - whole).astype(BF16)
    count = whole.astype(BF16)
    odd = count - ((count + BF16(384.0)) - BF16(384.0))
    a = (inv * inv).astype(BF16) * (BF16(1.0) - BF16(2.0) * (odd * odd))
    z = inv.astype(BF16) * BF16(1.0 / math.pi)
    u = part * part
    sine = part * (BF16(3.14064334) + u * (BF16(-5.13694906) + u * BF16(2.29967451)))
    cosine = BF16(0.99940325) + u * (BF16(-4.89118702) + u * BF16(3.58384395))
    return a * (sine + z * cosine), a * (cosine - z * sine)


def body(
    pos_hbm, ori_hbm, area_hbm, inc_hbm, vis_hbm, out_ref,
    pos_ref, ori_ref, area_ref, inc_ref, vis_ref, st_obs, rx_obs, st_pw, rx_pw, st_vis, rx_vis, st_cur, rx_cur, st_sum, rx_sum,
    inc_pack, obs_all, pw_all, right_t, right, left_f, left, s_a, s_b, k_all, x_near, x_far, acc,
    load_sem, send_sem, recv_sem,
):
    row, col = lax.axis_index("row"), lax.axis_index("col")
    x0, zl0 = lax.rem(row, NX), row // NX
    y0, zh0, c0 = col // 4, lax.rem(col // 2, 2), lax.rem(col, 2)
    z0 = zh0 * 4 + zl0

    def device(dx=0, dy=0, dz=0, dc=0):
        x, y, z, c = lax.rem(x0 + dx, NX), lax.rem(y0 + dy, NY), lax.rem(z0 + dz, NZ), lax.rem(c0 + dc, NC)
        return {"row": lax.rem(z, 4) * NX + x, "col": y * 4 + (z // 4) * 2 + c}

    loads = [
        pltpu.make_async_copy(src, dst, load_sem.at[i])
        for i, (src, dst) in enumerate(
            ((pos_hbm, pos_ref), (ori_hbm, ori_ref), (area_hbm, area_ref), (vis_hbm, vis_ref), (inc_hbm, inc_ref))
        )
    ]
    for load in loads:
        load.start()
    barrier = pltpu.get_barrier_semaphore()
    for x, z in XZ:
        pl.semaphore_signal(barrier, inc=1, device_id=device(dx=x, dz=z), device_id_type=MESH)
    for y, c in YC:
        pl.semaphore_signal(barrier, inc=1, device_id=device(dy=y, dc=c), device_id_type=MESH)

    lane = lax.broadcasted_iota(jnp.int32, (8, 128), 1)
    sub = lax.broadcasted_iota(jnp.int32, (8, 128), 0)
    low = lane < TILE
    top = sub < 4

    def swap_halves(v):
        return pltpu.roll(v, TILE, axis=1)

    def wide(v):
        return jnp.concatenate([v, jnp.zeros((v.shape[0], 128 - v.shape[1]), v.dtype)], axis=1)

    for load in loads:
        load.wait()

    pos = pos_ref[...]
    polar, azimuth = ori_ref[0:1, :], ori_ref[1:2, :]
    sin_p = jnp.sin(polar)
    st_obs[0] = jnp.zeros((8, 128), F32)
    st_obs[0, 0:3, 0:TILE] = pos
    st_obs[0, 3:4, 0:TILE] = sin_p * jnp.cos(azimuth)
    st_obs[0, 4:5, 0:TILE] = sin_p * jnp.sin(azimuth)
    st_obs[0, 5:6, 0:TILE] = jnp.cos(polar)
    st_obs[1] = swap_halves(st_obs[0])
    rx_obs[0] = st_obs[0]
    acc[0:8, 0:128] = jnp.zeros((8, 128), F32)
    acc[0:3, 0:TILE] = pos
    acc[3:4, 0:TILE] = area_ref[...] * (2.0 * 128.0 / math.sqrt(32768.0))
    own_pw = acc[0:8, 0:128]
    st_pw[0] = own_pw[0:4]
    st_pw[1] = swap_halves(own_pw)[0:4]
    rx_pw[0] = own_pw[0:4]
    st_vis[...] = jnp.concatenate([wide(vis_ref[b].astype(F32)) for b in range(16)], axis=0).astype(BF16)

    inc_pack[...] = jnp.zeros((8, 128), F32)
    for k in range(2):
        inc_pack[4 * k : 4 * k + 2, 0:TILE] = inc_ref[0, k]
        inc_pack[4 * k + 2 : 4 * k + 4, 0:TILE] = inc_ref[1, k]
    third = jnp.concatenate([inc_ref[0, 2], inc_ref[1, 2], jnp.zeros((4, TILE), F32)], axis=0)
    inc_pack[...] += swap_halves(wide(third))

    def stage_current(bounce, packed):
        st_cur[bounce, 0] = packed.astype(BF16)
        st_cur[bounce, 1] = swap_halves(packed).astype(BF16)
        rx_cur[bounce, 0] = st_cur[bounce, 0]

    stage_current(0, inc_pack[...])

    slot = lax.broadcasted_iota(jnp.int32, (32, 16), 0)
    there = lax.broadcasted_iota(jnp.int32, (32, 16), 1)
    place = slot // NX
    z_of = lax.rem(z0 + ring_offset(place), NZ)
    match = there == lax.rem(z_of, 4) * NX + lax.rem(x0 + lax.rem(slot, NX), NX)
    own_z = (z_of // 4) == zh0
    pick_own = jnp.where(match & own_z, 1.0, 0.0).astype(BF16)
    pick_far = jnp.where(match & jnp.logical_not(own_z), 1.0, 0.0).astype(BF16)
    a_row = lax.broadcasted_iota(jnp.int32, (128, NOBS), 0)
    a_lane = lax.broadcasted_iota(jnp.int32, (128, NOBS), 1)
    a_of = (
        lax.rem(y0 + ring_offset(a_lane // 128), NY) * 4 + zh0 * 2 + lax.rem(c0 + lax.rem(a_lane // TILE, 2), 2)
    )
    spread = jnp.where(a_row == a_of, 1.0, 0.0).astype(BF16)

    right_t[...] = jnp.zeros((DEPTH, NSRC), F32)
    right_t[18:24, :] = jnp.ones((6, NSRC), F32)
    b_row = lax.broadcasted_iota(jnp.int32, (32, NSRC), 0)
    b_lane = lax.broadcasted_iota(jnp.int32, (32, NSRC), 1)
    right_t[24:56, :] = jnp.where(b_row == b_lane // TILE, 1.0, 0.0)

    pl.semaphore_wait(barrier, len(XZ) + len(YC))

    def send(src, dst, sem, **offset):
        pltpu.make_async_remote_copy(
            src_ref=src, dst_ref=dst, send_sem=send_sem.at[sem], recv_sem=recv_sem.at[sem],
            device_id=device(**offset), device_id_type=MESH,
        ).start()

    def arrived(ref, sem):
        pltpu.make_async_copy(ref, ref, recv_sem.at[sem]).wait()

    def left_here(ref, sem):
        pltpu.make_async_copy(ref, ref, send_sem.at[sem]).wait()

    near_slots, far_slots = NEAR_Z * NX, (NZ - NEAR_Z) * NX
    S_OBS, S_VIS, S_PWN, S_PWF, S_CUR, S_SUM = 0, 1, 2, 3, 4, 10

    def sem_of(base, x, z):
        return base if src_slot(-x, -z) < near_slots else base + 1

    def send_place(x, z):
        send(st_pw.at[x % 2], rx_pw.at[src_slot(-x, -z)], sem_of(S_PWN, x, z), dx=x, dz=z)

    near_peers = [(x, z) for x, z in XZ if src_slot(-x, -z) < near_slots]
    far_peers = [(x, z) for x, z in XZ if src_slot(-x, -z) >= near_slots]

    send(st_vis, rx_vis, S_VIS, dz=4)
    for i in range(max(len(YC), len(near_peers))):
        if i < len(YC):
            y, c = YC[i]
            send(st_obs.at[c], rx_obs.at[obs_slot(-y, c)], S_OBS, dy=y, dc=c)
        if i < len(near_peers):
            send_place(*near_peers[i])
    for x, z in far_peers:
        send_place(x, z)

    def send_current(bounce):
        for x, z in XZ:
            send(
                st_cur.at[bounce, x % 2], rx_cur.at[bounce, src_slot(-x, -z)],
                sem_of(S_CUR + 2 * bounce, x, z), dx=x, dz=z,
            )

    send_current(0)

    arrived(rx_obs.at[pl.ds(1, NY * NC - 1)], S_OBS)
    for y in range(NY):
        obs_all[:, y * 128 : (y + 1) * 128] = rx_obs[2 * y] + rx_obs[2 * y + 1]
    big_pos = 8.0 * obs_all[0:3, :]
    h, m, l = split3(big_pos)
    for i, part in enumerate((h, m, l, h, m, h)):
        left_f[3 * i : 3 * i + 3, :] = part
    left_f[18:21, :] = jnp.ones((3, NOBS), F32)
    norms = split3(jnp.sum(big_pos * big_pos, axis=0, keepdims=True) + 64.0 * 0.0025)
    for i, part in enumerate(norms):
        left_f[21 + i : 22 + i, :] = part
    left_f[56:64, :] = jnp.zeros((8, NOBS), F32)

    def source_side(first, count):
        groups = range(first // 128, (first + count) // 128)
        for g in groups:
            pw_all[:, g * 128 : (g + 1) * 128] = rx_pw[2 * g] + rx_pw[2 * g + 1]
        span = slice(first, first + count)
        big_src = 8.0 * pw_all[0:3, span]
        h, m, l = split3(big_src)
        for i, part in enumerate((h, h, h, m, m, l)):
            right_t[3 * i : 3 * i + 3, span] = -2.0 * part
        norms = split3(jnp.sum(big_src * big_src, axis=0, keepdims=True))
        for i, part in enumerate(norms):
            right_t[18 + i : 19 + i, span] = part
        for g in groups:
            right[g * 128 : (g + 1) * 128, :] = jnp.transpose(right_t[:, g * 128 : (g + 1) * 128]).astype(BF16)

    arrived(rx_pw.at[pl.ds(1, near_slots - 1)], S_PWN)
    source_side(0, NEAR)
    arrived(rx_vis, S_VIS)
    seen = jnp.dot(pick_own, st_vis[...], preferred_element_type=F32) + jnp.dot(
        pick_far, rx_vis[...], preferred_element_type=F32
    )
    seen_all = jnp.dot(seen.astype(BF16), spread, preferred_element_type=F32)
    left_f[24:56, :] = BIG * (1.0 - seen_all)
    left[...] = left_f[...].astype(BF16)

    def operand(bounce, groups, first, x_ref):
        span = len(groups) * 128
        for g in groups:
            lanes = slice(g * 128, (g + 1) * 128)
            even, odd = rx_cur[bounce, 2 * g].astype(F32), rx_cur[bounce, 2 * g + 1].astype(F32)
            same = jnp.where(low, even, odd)
            s = (same, pltpu.roll(same, 4, axis=0), swap_halves(jnp.where(low, odd, even)))
            p = [pw_all[k : k + 1, lanes] for k in range(3)]
            w = pw_all[3:4, lanes]
            rows = []
            turned = []
            for k in range(3):
                i, j = (k + 1) % 3, (k + 2) % 3
                cross = p[i] * s[j] - p[j] * s[i]
                both = jnp.where(top, s[k], pltpu.roll(cross, 4, axis=0)) * w
                rows.append(both)
                turned.append(
                    jnp.where(lax.rem(sub, 4) < 2, -pltpu.roll(both, 6, axis=0), pltpu.roll(both, 2, axis=0))
                )
            at = (g - first) * 128
            for begin, parts in ((at, rows), (span + at, turned)):
                exact = jnp.concatenate(parts, axis=0)
                high = exact.astype(BF16)
                rest = (exact - high.astype(F32)).astype(BF16)
                x_ref[:, begin : begin + 128] = jnp.concatenate([high, rest], axis=0)

    near_groups = range(0, NEAR // 128)
    far_groups = range(NEAR // 128, NSRC // 128)

    def near_operand(bounce):
        arrived(rx_cur.at[bounce, pl.ds(1, near_slots - 1)], S_CUR + 2 * bounce)
        operand(bounce, near_groups, 0, x_near)

    def far_operand(bounce):
        arrived(rx_cur.at[bounce, pl.ds(near_slots, far_slots)], S_CUR + 2 * bounce + 1)
        operand(bounce, far_groups, NEAR // 128, x_far)

    def near_product(lanes):
        both = jnp.dot(x_near[...], k_all[0 : 2 * NEAR, lanes], preferred_element_type=F32)
        return both[0 : ROWS // 2] + both[ROWS // 2 : ROWS]

    def far_product(lanes):
        both = jnp.dot(x_far[...], k_all[2 * NEAR : 2 * NSRC, lanes], preferred_element_type=F32)
        return both[0 : ROWS // 2] + both[ROWS // 2 : ROWS]

    def messages(bounce, place, total):
        lanes = slice(place * 128, (place + 1) * 128)
        y = RING_ORDER[place]
        p = [obs_all[k : k + 1, lanes] for k in range(3)]
        n = [obs_all[3 + k : 4 + k, lanes] for k in range(3)]
        a = [total[8 * k : 8 * k + 8, :] for k in range(3)]
        d = [
            p[(k + 1) % 3] * a[(k + 2) % 3] - p[(k + 2) % 3] * a[(k + 1) % 3] - pltpu.roll(a[k], 4, axis=0)
            for k in range(3)
        ]
        s = [n[(k + 1) % 3] * d[(k + 2) % 3] - n[(k + 2) % 3] * d[(k + 1) % 3] for k in range(3)]
        pair = jnp.where(top, s[0], pltpu.roll(s[1], 4, axis=0))
        for c, packed in (
            (1, jnp.where(low, swap_halves(pair), s[2])),
            (0, jnp.where(low, pair, swap_halves(s[2]))),
        ):
            if place == 0 and c == 0:
                rx_sum[bounce, 0] = packed.astype(BF16)
            else:
                st_sum[bounce, 2 * place + c] = packed.astype(BF16)
                send(
                    st_sum.at[bounce, 2 * place + c], rx_sum.at[bounce, obs_slot(-y, c)],
                    S_SUM + bounce, dy=y, dc=c,
                )

    def squares(block, lanes, ref):
        rows = pl.ds(aligned(block * BLOCK, BLOCK), BLOCK)
        ref[:, 0 : lanes.size] = jnp.dot(right[rows, :], left[:, lanes], preferred_element_type=F32)

    def fill(ref, block, lanes):
        near = block < NEAR // BLOCK
        re_row = aligned(block * BLOCK + either(near, 0, NEAR), BLOCK)
        im_row = aligned(block * BLOCK + either(near, NEAR, NSRC), BLOCK)
        for r in range(0, BLOCK, 16):
            for v in range(0, lanes.size, 256):
                re, im = pair_kernel(ref[r : r + 16, v : v + 256])
                at = pl.ds(aligned(lanes.start + v, BLOCK), BLOCK)
                k_all[pl.ds(re_row + r, 16), at] = re
                k_all[pl.ds(im_row + r, 16), at] = im

    def sweep(unit, count, last):
        squares(*unit(0), s_a)

        def two(i, _):
            squares(*unit(2 * i + 1), s_b)
            fill(s_a, *unit(2 * i))
            squares(*unit(jnp.minimum(2 * i + 2, last)), s_a)
            fill(s_b, *unit(2 * i + 1))
            return 0

        lax.fori_loop(0, count // 2, two, 0)

    near_blocks, far_blocks = NEAR // BLOCK, FAR // BLOCK
    sweep(
        lambda k: (k // 2, pl.ds(pl.multiple_of(lax.rem(k, 2) * HALF, HALF), HALF)),
        2 * near_blocks - 2, 2 * near_blocks - 3,
    )
    near_operand(0)
    last_near = [(near_blocks - 1, pl.ds(h * HALF, HALF)) for h in (0, 1)]
    squares(*last_near[0], s_a)
    squares(*last_near[1], s_b)
    arrived(rx_pw.at[pl.ds(near_slots, far_slots)], S_PWF)
    source_side(NEAR, FAR)
    fill(s_a, *last_near[0])
    far_operand(0)
    fill(s_b, *last_near[1])

    def finish(bounce, q):
        lanes = slice(q * BLOCK, (q + 1) * BLOCK)
        total = acc[:, lanes] + far_product(lanes)
        for place in (2 * q + 1, 2 * q):
            messages(bounce, place, total[:, (place % 2) * 128 : (place % 2) * 128 + 128])

    for h in (1, 0):
        units = [
            (near_blocks + b, pl.ds(h * HALF + q * BLOCK, BLOCK)) for q in (1, 0) for b in range(far_blocks)
        ]
        stages = (s_a, s_b)
        squares(*units[0], s_a)
        for k, unit in enumerate(units):
            if k + 1 < len(units):
                squares(*units[k + 1], stages[(k + 1) % 2])
            if k % far_blocks == 0:
                q = 2 * h + 1 - k // far_blocks
                acc[:, q * BLOCK : (q + 1) * BLOCK] = near_product(slice(q * BLOCK, (q + 1) * BLOCK))
            fill(stages[k % 2], *unit)
            if k % far_blocks == far_blocks - 1:
                finish(0, 2 * h + 1 - k // far_blocks)

    def sent_earlier():
        left_here(rx_obs.at[pl.ds(1, NY * NC - 1)], S_OBS)
        left_here(rx_vis, S_VIS)
        left_here(rx_pw.at[pl.ds(1, near_slots - 1)], S_PWN)
        left_here(rx_pw.at[pl.ds(near_slots, far_slots)], S_PWF)
        for bounce in range(ITERS):
            left_here(rx_cur.at[bounce, pl.ds(1, near_slots - 1)], S_CUR + 2 * bounce)
            left_here(rx_cur.at[bounce, pl.ds(near_slots, far_slots)], S_CUR + 2 * bounce + 1)
            if bounce < ITERS - 1:
                left_here(rx_sum.at[bounce, pl.ds(1, NY * NC - 1)], S_SUM + bounce)

    current = None
    for bounce in range(ITERS):
        if bounce > 0:
            near_operand(bounce)
            for h in (1, 0):
                acc[:, h * HALF : (h + 1) * HALF] = near_product(slice(h * HALF, (h + 1) * HALF))
            far_operand(bounce)
            for q in (3, 2, 1, 0):
                finish(bounce, q)
        if bounce == ITERS - 1:
            sent_earlier()
        arrived(rx_sum.at[bounce, pl.ds(1, NY * NC - 1)], S_SUM + bounce)
        current = inc_pack[...] + jnp.sum(rx_sum[bounce].astype(F32), axis=0)
        if bounce + 1 < ITERS:
            stage_current(bounce + 1, current)
            send_current(bounce + 1)

    third = swap_halves(current)
    for part in range(2):
        for k in range(2):
            out_ref[part, k] = current[4 * k + 2 * part : 4 * k + 2 * part + 2, 0:TILE]
        out_ref[part, 2] = third[2 * part : 2 * part + 2, 0:TILE]
    left_here(rx_sum.at[ITERS - 1, pl.ds(1, NY * NC - 1)], S_SUM + ITERS - 1)


def shards(positions, orient, areas, incident, visible):
    vmem = pltpu.VMEM
    scratch = [
        vmem((3, TILE), F32), vmem((2, TILE), F32), vmem((1, TILE), F32), vmem(incident.shape, F32),
        vmem((16, 1, 32), jnp.int32),
        vmem((2, 8, 128), F32), vmem((16, 8, 128), F32),
        vmem((2, 4, 128), F32), vmem((32, 4, 128), F32),
        vmem((16, 128), BF16), vmem((16, 128), BF16),
        vmem((ITERS, 2, 8, 128), BF16), vmem((ITERS, 32, 8, 128), BF16),
        vmem((ITERS, 16, 8, 128), BF16), vmem((ITERS, 16, 8, 128), BF16),
        vmem((8, 128), F32), vmem((8, NOBS), F32), vmem((4, NSRC), F32),
        vmem((DEPTH, NSRC), F32), vmem((NSRC, DEPTH), BF16), vmem((DEPTH, NOBS), F32), vmem((DEPTH, NOBS), BF16),
        vmem((BLOCK, HALF), F32), vmem((BLOCK, HALF), F32),
        vmem((2 * NSRC, NOBS), BF16),
        vmem((ROWS, 2 * NEAR), BF16), vmem((ROWS, 2 * FAR), BF16), vmem((ROWS // 2, NOBS), F32),
        pltpu.SemaphoreType.DMA((5,)), pltpu.SemaphoreType.DMA((13,)), pltpu.SemaphoreType.DMA((13,)),
    ]
    return pl.pallas_call(
        body,
        out_shape=jax.ShapeDtypeStruct(incident.shape, F32),
        in_specs=[pl.BlockSpec(memory_space=pl.ANY)] * 5,
        out_specs=pl.BlockSpec(memory_space=vmem),
        scratch_shapes=scratch,
        compiler_params=pltpu.CompilerParams(
            collective_id=0, has_side_effects=True, vmem_limit_bytes=60 * 2**20
        ),
        cost_estimate=pl.CostEstimate(flops=3_000_000_000, bytes_accessed=1_000_000, transcendentals=4_000_000),
    )(positions, orient, areas.reshape(1, -1), incident, jnp.transpose(visible, (1, 2, 0)))


def solution(mesh):
    in_specs = (
        P(None, ("row", "col")),
        P(None, ("row", "col")),
        P(("row", "col")),
        P(None, None, None, ("row", "col")),
        P("row", None, "col"),
    )
    out_specs = P(None, None, None, ("row", "col"))
    return jax.shard_map(shards, mesh=mesh, in_specs=in_specs, out_specs=out_specs, check_vma=False)
```
